128 devices in a mesh: seq: 32 (over y, z, core), ch: 4 (over x).
Axes of the slice: x: 4, y: 4, z: 4, core: 2. Of those that a mesh axis runs over, the one named last changes fastest.
Arguments:
- gate_in: bfloat16 [8192, 4096], P('seq', 'ch'), may hold values from -80 to 80
- key_in: bfloat16 [8192, 4096], P('seq', 'ch'), may hold values from -6 to 6
- value_in: bfloat16 [8192, 4096], P('seq', 'ch'), may hold values from -6 to 6
- long_filter: bfloat16 [8192, 4096], P('seq', 'ch'), may hold values from -2 to 2
- gate_short: float32 [3, 4096], P(None, 'ch'), may hold values from -3 to 3
- key_short: float32 [3, 4096], P(None, 'ch'), may hold values from -3 to 3
- value_short: float32 [3, 4096], P(None, 'ch'), may hold values from -3 to 3
- skip_gain: float32 [4096], P('ch'), may hold values from 0.5 to 1.5
- norm_gain: float32 [4096], P('ch'), may hold values from 0.5 to 1.5
Outputs:
- mixed: bfloat16 [8192, 4096], P('seq', 'ch')
The draws below stay inside these ranges and needn't reach their ends.
All inputs are finite; a program needn't handle non-finite values.
Results may differ from the reference program's by a relative error of at most 0.0057.
Values may be sent and summed in bfloat16 or wider, within the bound.
A program may use at most 64 MiB of HBM per device.

```python
import math
import jax
import jax.numpy as jnp
from jax import lax

D = 4096
TAPS = 3
SEQLEN = 8192


def draw_gate_in(key, part):
    first, second, third = jax.random.split(key, 3)
    rowscale = jnp.exp(jax.random.uniform(second, (SEQLEN, 1), minval=0.0, maxval=math.log(10.0)))
    spread = jax.random.uniform(third, (1, D))
    ramp = jnp.arange(D, dtype=jnp.float32)[None, :] / D
    base = jax.random.normal(first, (SEQLEN, D))
    colscale = 10.0 ** (0.6 * ramp + 0.4 * spread)
    return jnp.clip(base * rowscale * colscale / 10.0, -70.0, 70.0).astype(jnp.bfloat16)


def draw_long_filter(key, part):
    key = jax.random.fold_in(key, 7)
    first, second, third, fourth, fifth = jax.random.split(key, 5)
    lags = jnp.arange(SEQLEN, dtype=jnp.float32)[:, None]
    choose = jax.random.uniform(second, (1, D))
    slow_tau = jnp.exp(jax.random.uniform(third, (1, D), minval=math.log(SEQLEN / 2.0), maxval=math.log(20.0 * SEQLEN)))
    fast_tau = jnp.exp(jax.random.uniform(fourth, (1, D), minval=math.log(20.0), maxval=math.log(200.0)))
    decay = jnp.where(choose < 0.5, slow_tau, fast_tau)
    amplitude = 0.8 / jnp.sqrt(jnp.minimum(decay, float(SEQLEN)))
    tail_amp = 0.2 / math.sqrt(float(SEQLEN))
    noise = jnp.clip(jax.random.normal(first, (SEQLEN, D)), -6.0, 6.0)
    tail = jnp.clip(jax.random.normal(fifth, (SEQLEN, D)), -6.0, 6.0)
    taps = noise * amplitude * jnp.exp(-lags / decay) + tail_amp * tail
    return jnp.clip(taps, -1.9, 1.9).astype(jnp.bfloat16)


def shard_levels(stream_key, dims, cuts, smallest, largest):
    loudness, own = 1.0, jax.random.fold_in(stream_key, 6)
    for axis_at, blocks in cuts:
        steps = jnp.exp(jax.random.uniform(jax.random.fold_in(own, axis_at), (blocks,), jnp.float32, smallest / len(cuts), largest / len(cuts)))
        loudness = loudness * jnp.repeat(steps, dims[axis_at] // blocks).reshape([-1 if axis == axis_at else 1 for axis in range(len(dims))])
    return loudness


def centred(own_key, dims, scale, limit, cuts=(), kind=jnp.bfloat16):
    values = scale * jax.random.normal(own_key, dims, jnp.float32)
    if cuts:
        values = values * shard_levels(own_key, dims, cuts, -0.22, 0.18)
    return jnp.clip(values, -limit, limit).astype(kind)


def setup_inputs(seed: int = 0) -> dict:
    seeds = jax.random.split(jax.random.key(seed), 10)
    gate_in = draw_gate_in(jax.random.fold_in(seeds[9], 71), 0)
    key_in = centred(seeds[1], (SEQLEN, D), 1.0, 6.0, ((0, 32), (1, 4)))
    value_in = centred(seeds[2], (SEQLEN, D), 1.0, 6.0, ((0, 32), (1, 4)))
    long_filter = draw_long_filter(jax.random.fold_in(seeds[9], 71), 0)
    gate_short = centred(seeds[4], (TAPS, D), 0.7, 3.0, ((1, 4),), jnp.float32)
    key_short = centred(seeds[5], (TAPS, D), 0.7, 3.0, ((1, 4),), jnp.float32)
    value_short = centred(seeds[6], (TAPS, D), 0.7, 3.0, ((1, 4),), jnp.float32)
    skip_gain = jnp.clip(0.5 + 1.0 * jax.random.uniform(seeds[7], (D,), jnp.float32) ** shard_levels(seeds[7], (D,), ((0, 4),), -0.2, 0.2), 0.5, 1.5)
    norm_gain = jnp.clip(1.0 + 0.1 * jax.random.normal(seeds[8], (D,), jnp.float32), 0.5, 1.5)
    return {"gate_in": gate_in, "key_in": key_in, "value_in": value_in, "long_filter": long_filter, "gate_short": gate_short, "key_short": key_short, "value_short": value_short, "skip_gain": skip_gain, "norm_gain": norm_gain}


def short_conv(rows, taps):
    padded = jnp.pad(rows, ((2, 0), (0, 0)))
    return taps[0] * rows + taps[1] * padded[1:-1] + taps[2] * padded[:-2]

def lane_conv(pair):
    left, right = pair
    left_spec = jnp.fft.rfft(left, n=2 * SEQLEN, axis=0)
    right_spec = jnp.fft.rfft(right, n=2 * SEQLEN, axis=0)
    return jnp.fft.irfft(left_spec * right_spec, n=2 * SEQLEN, axis=0)[:SEQLEN]

def reference(gate_in, key_in, value_in, long_filter, gate_short, key_short, value_short, skip_gain, norm_gain):
    gate_conv = short_conv(gate_in.astype(jnp.float32), gate_short.astype(jnp.float32))
    key_conv = short_conv(key_in.astype(jnp.float32), key_short.astype(jnp.float32))
    value_conv = short_conv(value_in.astype(jnp.float32), value_short.astype(jnp.float32))
    product = (key_conv * value_conv).astype(jnp.bfloat16)
    width = math.gcd(D, 256)
    blocks = D // width
    left = product.astype(jnp.float32).reshape(SEQLEN, blocks, width).transpose(1, 0, 2)
    right = long_filter.astype(jnp.float32).reshape(SEQLEN, blocks, width).transpose(1, 0, 2)
    conv = lax.map(lane_conv, (left, right)).transpose(1, 0, 2).reshape(SEQLEN, D)
    mixed_in = (conv + skip_gain.astype(jnp.float32)[None, :] * product.astype(jnp.float32)).astype(jnp.bfloat16)
    gated = gate_conv * mixed_in.astype(jnp.float32)
    meansq = lax.optimization_barrier(jnp.mean(gated * gated, axis=1, keepdims=True))
    return (gated * norm_gain.astype(jnp.float32)[None, :] * lax.rsqrt(meansq + 1e-06)).astype(jnp.bfloat16)
```

```python
import functools

import jax
import jax.numpy as jnp
from jax import lax
from jax.experimental import pallas as pl
from jax.experimental.pallas import tpu as pltpu
from jax.sharding import PartitionSpec as P

MESH = pl.DeviceIdType.MESH
F32, BF = jnp.float32, jnp.bfloat16
NT = (((1,), (1,)), ((), ()))

BLOCKS = 32
GROUPS = 4
TOK = 256
WIDTH = 1024
PARTS = 4
C = 8
SLOTS = 2
LANES = 128
SEGS = 64
ROWS = SEGS * C


def peer_at(me, step):
    y, z, core = me // 8, lax.rem(me // 2, 4), lax.rem(me, 2)
    return (
        lax.rem(y + step // 8, 4) * 8
        + lax.rem(z + lax.rem(step // 2, 4), 4) * 2
        + lax.rem(core + lax.rem(step, 2), 2)
    )


def exchange(me, ch, src, dst, part, send_sem, recv_sem):
    mine = pl.ds(pl.multiple_of(me * 16, 16), 16)
    pltpu.make_async_copy(src.at[part, mine], dst.at[part, mine], recv_sem.at[part]).start()

    def send(step, carry):
        peer = peer_at(me, step)
        pltpu.make_async_remote_copy(
            src_ref=src.at[part, pl.ds(pl.multiple_of(peer * 16, 16), 16)],
            dst_ref=dst.at[part, mine],
            send_sem=send_sem.at[part],
            recv_sem=recv_sem.at[part],
            device_id=(peer, ch),
            device_id_type=MESH,
        ).start()
        return carry

    lax.fori_loop(1, BLOCKS, send, 0)


def arrived(dst, part, recv_sem):
    pltpu.make_async_copy(dst.at[part], dst.at[part], recv_sem.at[part]).wait()


def sent(src, part, send_sem):
    piece = src.at[part, pl.ds(0, 16 * (BLOCKS - 1))]
    pltpu.make_async_copy(piece, piece, send_sem.at[part]).wait()


def lanes_of(block):
    return pl.ds(pl.multiple_of(block * LANES, LANES), LANES)


def short_conv(full, taps, block):
    at = lanes_of(block)
    return (
        taps[0:1, at] * full[8 : 8 + TOK, at]
        + taps[1:2, at] * full[7 : 7 + TOK, at]
        + taps[2:3, at] * full[6 : 6 + TOK, at]
    )


def split_rows(tokens, block, dst):
    first, second = tokens[:LANES].T, tokens[LANES:].T
    for group in range(LANES // C):
        rows = slice(C * group, C * group + C)
        pair = jnp.concatenate([first[rows], second[rows]], axis=0).astype(BF)
        owner = block * 4 + group // PARTS
        dst[group % PARTS, pl.ds(pl.multiple_of(owner * 16, 16), 16), :] = pair


def make_left(c, slot, taps, left):
    lane = lax.broadcasted_iota(jnp.int32, (8, LANES), 1)
    for u in range(8):
        here = taps[pl.ds((1 + 8 * u) * C + c, 8, stride=C), :]
        before = taps[pl.ds(8 * u * C + c, 8, stride=C), :]
        phases = []
        for r in range(4):
            by = 32 * (3 - r)
            if by:
                phases.append(pltpu.roll(jnp.where(lane >= LANES - by, before, here), by, 1))
            else:
                phases.append(here)
        left[slot, 32 + 32 * u : 64 + 32 * u, :] = jnp.concatenate(phases, axis=0).astype(BF)


def make_right(c, slot, flipped, right):
    lane = lax.broadcasted_iota(jnp.int32, (8, LANES), 1)
    row = lax.broadcasted_iota(jnp.int32, (8, LANES), 0)
    masks = [lane < 31 - 8 * o - row for o in range(4)]
    before = jnp.broadcast_to(flipped[pl.ds(c, 1), :], (8, LANES))
    for m in range(SEGS):
        b, g = m // 8, m % 8
        here = jnp.broadcast_to(flipped[pl.ds((m + 1) * C + c, 1), :], (8, LANES))
        phases = [
            pltpu.roll(
                jnp.where(masks[o], before, here), 97 + 8 * o, 1, stride=1, stride_axis=0
            )
            for o in range(4)
        ]
        half = LANES * (b % 2)
        right[slot, b // 2, 32 * g : 32 * g + 32, half : half + LANES] = jnp.concatenate(
            phases, axis=0
        ).astype(BF)
        before = here


def multiply(slot, left, right, sums):
    total = None
    for k in range(4):
        n = 256 - 64 * k
        lhs = jnp.concatenate([left[slot, 32 : 32 + n, :], left[slot, 0:n, :]], axis=1)
        part = lax.dot_general(lhs, right[slot, k], NT, preferred_element_type=F32)
        if total is None:
            total = [part[64 * i : 64 * i + 64] for i in range(4)]
        else:
            for i in range(k, 4):
                total[i] = total[i] + part[64 * (i - k) : 64 * (i - k) + 64]
    for u in range(8):
        for r in range(4):
            at = 32 * (u % 2) + 8 * r
            sums[slot, r, 8 + 8 * u : 16 + 8 * u, :] = total[u // 2][at : at + 8]


def fold(c, slot, skip, sums, plain, result):
    lane = lax.broadcasted_iota(jnp.int32, (8, LANES), 1)
    for u in range(8):
        y = None
        for d in range(4):
            v = None
            for j in range(4):
                r = (j + d) % 4
                low = sums[slot, r, 8 + 8 * u - j : 16 + 8 * u - j, 0:LANES]
                high = sums[slot, r, 4 + 8 * u - j : 12 + 8 * u - j, LANES : 2 * LANES]
                w = low + high
                v = w if v is None else jnp.where(lane >= 32 * j, w, v)
            if d:
                v = pltpu.roll(v, 32 * d, 1)
            y = v if y is None else y + v
        at = pl.ds(8 * u * C + c, 8, stride=C)
        result[at, :] = y + skip * plain[at, :]


def kernel(
    gate_hbm, key_hbm, value_hbm, filter_hbm,
    gate_short, key_short, value_short, skip_gain, norm_gain,
    out, scale,
    gate_in, key_in, value_in, filter_in, load_sem,
    gate_full, key_full, value_full,
    edge_out, edge_in, edge_send, edge_recv,
    filter_send, filter_recv, product_send, product_recv, mixed_send, mixed_recv,
    sems,
    gated, taps, plain, flipped, result, left, right, sums,
    square_send, square_recv, square_sems,
):
    me, ch = lax.axis_index("seq"), lax.axis_index("ch")
    loads = [
        pltpu.make_async_copy(src, dst, load_sem.at[i])
        for i, (src, dst) in enumerate(
            ((key_hbm, key_in), (value_hbm, value_in), (gate_hbm, gate_in), (filter_hbm, filter_in))
        )
    ]
    for load in loads:
        load.start()

    barrier = pltpu.get_barrier_semaphore()

    def greet(step, carry):
        pl.semaphore_signal(
            barrier, inc=1, device_id=(peer_at(me, step), ch), device_id_type=MESH
        )
        return carry

    lax.fori_loop(1, BLOCKS, greet, 0)
    for d in range(1, GROUPS):
        pl.semaphore_signal(
            barrier, inc=1, device_id=(me, lax.rem(ch + d, GROUPS)), device_id_type=MESH
        )

    for load in loads[:3]:
        load.wait()
    edge_out[...] = jnp.zeros_like(edge_out)
    for i, (src, full) in enumerate(
        ((key_in, key_full), (value_in, value_full), (gate_in, gate_full))
    ):
        full[8 : 8 + TOK, :] = src[...].astype(F32)
        edge_out[2 * i : 2 * i + 2, :] = full[6 + TOK : 8 + TOK, :]

    pl.semaphore_wait(barrier, BLOCKS - 1 + GROUPS - 1)
    edge = pltpu.make_async_remote_copy(
        src_ref=edge_out,
        dst_ref=edge_in,
        send_sem=edge_send,
        recv_sem=edge_recv,
        device_id=(lax.rem(me + 1, BLOCKS), ch),
        device_id_type=MESH,
    )
    edge.start()
    loads[3].wait()

    def cut_filter(block, carry):
        split_rows(filter_in[:, lanes_of(block)].astype(F32), block, filter_send)
        return carry

    lax.fori_loop(0, WIDTH // LANES, cut_filter, 0)
    filter_sems, product_sems, mixed_sems = (
        (sems.at[2 * i], sems.at[2 * i + 1]) for i in range(3)
    )
    exchange(me, ch, filter_send, filter_recv, 0, *filter_sems)

    edge.wait()
    for i, full in enumerate((key_full, value_full, gate_full)):
        full[6:8, :] = jnp.where(me == 0, 0.0, edge_in[2 * i : 2 * i + 2, :])

    def cut_product(block, carry):
        product = short_conv(key_full, key_short, block) * short_conv(
            value_full, value_short, block
        )
        split_rows(product.astype(BF).astype(F32), block, product_send)
        return carry

    lax.fori_loop(0, WIDTH // LANES, cut_product, 0)
    exchange(me, ch, product_send, product_recv, 0, *product_sems)

    def exchange_both(part, carry):
        exchange(me, ch, filter_send, filter_recv, part, *filter_sems)
        exchange(me, ch, product_send, product_recv, part, *product_sems)
        return carry

    lax.fori_loop(1, PARTS, exchange_both, 0)

    def turn_gate(block, carry):
        gate = short_conv(gate_full, gate_short, block)
        gated[lanes_of(block), 0:LANES] = gate[:LANES].T
        gated[lanes_of(block), LANES : 2 * LANES] = gate[LANES:].T
        return carry

    lax.fori_loop(0, WIDTH // LANES, turn_gate, 0)

    taps[0:C, :] = jnp.zeros((C, LANES), F32)
    flipped[0:C, :] = jnp.zeros((C, LANES), F32)
    for slot in range(SLOTS):
        left[slot, 0:32, :] = jnp.zeros((32, LANES), BF)
        for r in range(4):
            sums[slot, r, 0:8, :] = jnp.zeros((8, 2 * LANES), F32)
    rows = lax.broadcasted_iota(jnp.int32, (LANES, LANES), 0)
    cols = lax.broadcasted_iota(jnp.int32, (LANES, LANES), 1)
    flip = jnp.where(rows + cols == LANES - 1, 1.0, 0.0).astype(BF)

    def convolve(part, carry):
        arrived(filter_recv, part, filter_sems[1])
        taps[C:, :] = filter_recv[part].astype(F32)
        arrived(product_recv, part, product_sems[1])
        plain[...] = product_recv[part].astype(F32)
        flipped[C:, :] = jnp.dot(product_recv[part], flip, preferred_element_type=F32)

        def channels(i, carry):
            for slot in range(SLOTS):
                c = i * SLOTS + slot
                make_left(c, slot, taps, left)
                make_right(c, slot, flipped, right)
                multiply(slot, left, right, sums)
                skip = skip_gain[me * (PARTS * C) + part * C + c]
                fold(c, slot, skip, sums, plain, result)
            return carry

        lax.fori_loop(0, C // SLOTS, channels, 0)
        mixed_send[part] = result[...].astype(BF)
        exchange(me, ch, mixed_send, mixed_recv, part, *mixed_sems)
        return carry

    lax.fori_loop(0, PARTS, convolve, 0)

    def gate_part(part, squares):
        arrived(mixed_recv, part, mixed_sems[1])

        def gate_owner(owner, squares):
            pair = mixed_recv[part, pl.ds(pl.multiple_of(owner * 16, 16), 16), :].astype(F32)
            at = pl.ds(pl.multiple_of(owner * (PARTS * C) + part * C, C), C)
            g = gated[at, :] * jnp.concatenate([pair[:C], pair[C:]], axis=1)
            gated[at, :] = g
            return squares + g * g

        return lax.fori_loop(0, BLOCKS, gate_owner, squares, unroll=4)

    squares = lax.fori_loop(0, PARTS, gate_part, jnp.zeros((C, TOK), F32))
    square_send[...] = squares
    tells = [
        pltpu.make_async_remote_copy(
            src_ref=square_send,
            dst_ref=square_recv.at[d - 1],
            send_sem=square_sems.at[0, d - 1],
            recv_sem=square_sems.at[1, d - 1],
            device_id=(me, lax.rem(ch + d, GROUPS)),
            device_id_type=MESH,
        )
        for d in range(1, GROUPS)
    ]
    for tell in tells:
        tell.start()

    def turn_back(block, carry):
        at = lanes_of(block)
        out[:, at] = gated[at, :].T * norm_gain[0:1, at]
        return carry

    lax.fori_loop(0, WIDTH // LANES, turn_back, 0)
    for tell in tells:
        tell.wait()
    for d in range(GROUPS - 1):
        squares = squares + square_recv[d]
    meansq = jnp.sum(squares, axis=0, keepdims=True) / (WIDTH * GROUPS)
    inverse = lax.rsqrt(meansq + 1e-06)
    scale[...] = jnp.broadcast_to(inverse, (LANES, TOK)).T

    edge_free = [(filter_send, filter_sems), (product_send, product_sems), (mixed_send, mixed_sems)]
    for src, pair in edge_free:
        for part in range(PARTS):
            sent(src, part, pair[0])


def local(
    gate_in, key_in, value_in, long_filter, gate_short, key_short, value_short, skip_gain, norm_gain
):
    vmem = pl.BlockSpec(memory_space=pltpu.VMEM)
    smem = pl.BlockSpec(memory_space=pltpu.SMEM)
    hbm = pl.BlockSpec(memory_space=pl.ANY)
    parts = (PARTS, ROWS, LANES)
    gated, scale = pl.pallas_call(
        kernel,
        out_shape=(
            jax.ShapeDtypeStruct((TOK, WIDTH), F32),
            jax.ShapeDtypeStruct((TOK, LANES), F32),
        ),
        in_specs=[hbm] * 4 + [vmem] * 3 + [smem, vmem],
        out_specs=(vmem, vmem),
        scratch_shapes=[
            *[pltpu.VMEM((TOK, WIDTH), BF)] * 4,
            pltpu.SemaphoreType.DMA((4,)),
            *[pltpu.VMEM((8 + TOK, WIDTH), F32)] * 3,
            *[pltpu.VMEM((8, WIDTH), F32)] * 2,
            pltpu.SemaphoreType.DMA,
            pltpu.SemaphoreType.DMA,
            *[pltpu.VMEM(parts, BF)] * 6,
            pltpu.SemaphoreType.DMA((6, PARTS)),
            pltpu.VMEM((WIDTH, TOK), F32),
            pltpu.VMEM((ROWS + C, LANES), F32),
            pltpu.VMEM((ROWS, LANES), F32),
            pltpu.VMEM((ROWS + C, LANES), F32),
            pltpu.VMEM((ROWS, LANES), F32),
            pltpu.VMEM((SLOTS, 288, LANES), BF),
            pltpu.VMEM((SLOTS, 4, 256, 256), BF),
            pltpu.VMEM((SLOTS, 4, 72, 256), F32),
            pltpu.VMEM((C, TOK), F32),
            pltpu.VMEM((GROUPS - 1, C, TOK), F32),
            pltpu.SemaphoreType.DMA((2, GROUPS - 1)),
        ],
        compiler_params=pltpu.CompilerParams(
            collective_id=0, has_side_effects=True, vmem_limit_bytes=60 << 20
        ),
        name="hyena",
    )(
        gate_in, key_in, value_in, long_filter,
        gate_short, key_short, value_short, skip_gain, norm_gain.reshape(1, WIDTH),
    )
    return (gated * scale[:, :1]).astype(BF)


def solution(mesh):
    return jax.shard_map(
        local,
        mesh=mesh,
        in_specs=(
            P("seq", "ch"),
            P("seq", "ch"),
            P("seq", "ch"),
            P("seq", "ch"),
            P(None, "ch"),
            P(None, "ch"),
            P(None, "ch"),
            P("ch"),
            P("ch"),
        ),
        out_specs=P("seq", "ch"),
        check_vma=False,
    )
```

```python
import functools

import jax
import jax.numpy as jnp
from jax import lax
from jax.experimental import pallas as pl
from jax.experimental.pallas import tpu as pltpu
from jax.sharding import PartitionSpec as P

MESH = pl.DeviceIdType.MESH
F32, BF = jnp.float32, jnp.bfloat16
NT = (((1,), (1,)), ((), ()))

BLOCKS = 32
GROUPS = 4
TOK = 256
WIDTH = 1024
PARTS = 4
C = 8
SLOTS = 2
LANES = 128
SEGS = 64
ROWS = SEGS * C


def others(me):
    ys = [lax.rem(me // 8 + d, 4) * 8 for d in range(4)]
    zs = [lax.rem(me // 2 + d, 4) * 2 for d in range(4)]
    cores = [lax.rem(me + d, 2) for d in range(2)]
    return [y + z + core for y in ys for z in zs for core in cores][1:]


def exchange(me, ch, peers, src, dst, part, send_sem, recv_sem):
    mine = pl.ds(pl.multiple_of(me * 16, 16), 16)
    pltpu.make_async_copy(src.at[part, mine], dst.at[part, mine], recv_sem.at[part]).start()
    for peer in peers:
        pltpu.make_async_remote_copy(
            src_ref=src.at[part, pl.ds(pl.multiple_of(peer * 16, 16), 16)],
            dst_ref=dst.at[part, mine],
            send_sem=send_sem.at[part],
            recv_sem=recv_sem.at[part],
            device_id=(peer, ch),
            device_id_type=MESH,
        ).start()


def arrived(dst, part, recv_sem):
    pltpu.make_async_copy(dst.at[part], dst.at[part], recv_sem.at[part]).wait()


def sent(src, part, send_sem):
    piece = src.at[part, pl.ds(0, 16 * (BLOCKS - 1))]
    pltpu.make_async_copy(piece, piece, send_sem.at[part]).wait()


def lanes_of(block):
    return pl.ds(pl.multiple_of(block * LANES, LANES), LANES)


def short_conv(full, taps, block):
    at = lanes_of(block)
    return (
        taps[0:1, at] * full[8 : 8 + TOK, at]
        + taps[1:2, at] * full[7 : 7 + TOK, at]
        + taps[2:3, at] * full[6 : 6 + TOK, at]
    )


def split_rows(tokens, block, dst):
    first, second = tokens[:LANES].T, tokens[LANES:].T
    for group in range(LANES // C):
        rows = slice(C * group, C * group + C)
        pair = jnp.concatenate([first[rows], second[rows]], axis=0).astype(BF)
        owner = block * 4 + group // PARTS
        dst[group % PARTS, pl.ds(pl.multiple_of(owner * 16, 16), 16), :] = pair


def make_left(c, slot, taps, left):
    lane = lax.broadcasted_iota(jnp.int32, (8, LANES), 1)
    for u in range(8):
        here = taps[pl.ds((1 + 8 * u) * C + c, 8, stride=C), :]
        before = taps[pl.ds(8 * u * C + c, 8, stride=C), :]
        phases = []
        for r in range(4):
            by = 32 * (3 - r)
            if by:
                phases.append(pltpu.roll(jnp.where(lane >= LANES - by, before, here), by, 1))
            else:
                phases.append(here)
        left[slot, 32 + 32 * u : 64 + 32 * u, :] = jnp.concatenate(phases, axis=0).astype(BF)


def make_right(c, slot, flipped, right):
    lane = lax.broadcasted_iota(jnp.int32, (8, LANES), 1)
    row = lax.broadcasted_iota(jnp.int32, (8, LANES), 0)
    masks = [lane < 31 - 8 * o - row for o in range(4)]
    before = jnp.broadcast_to(flipped[pl.ds(c, 1), :], (8, LANES))
    for m in range(SEGS):
        b, g = m // 8, m % 8
        here = jnp.broadcast_to(flipped[pl.ds((m + 1) * C + c, 1), :], (8, LANES))
        phases = [
            pltpu.roll(
                jnp.where(masks[o], before, here), 97 + 8 * o, 1, stride=1, stride_axis=0
            )
            for o in range(4)
        ]
        half = LANES * (b % 2)
        right[slot, b // 2, 32 * g : 32 * g + 32, half : half + LANES] = jnp.concatenate(
            phases, axis=0
        ).astype(BF)
        before = here


def multiply(slot, left, right, sums):
    total = None
    for k in range(4):
        n = 256 - 64 * k
        lhs = jnp.concatenate([left[slot, 32 : 32 + n, :], left[slot, 0:n, :]], axis=1)
        part = lax.dot_general(lhs, right[slot, k], NT, preferred_element_type=F32)
        if total is None:
            total = [part[64 * i : 64 * i + 64] for i in range(4)]
        else:
            for i in range(k, 4):
                total[i] = total[i] + part[64 * (i - k) : 64 * (i - k) + 64]
    for u in range(8):
        for r in range(4):
            at = 32 * (u % 2) + 8 * r
            sums[slot, r, 8 + 8 * u : 16 + 8 * u, :] = total[u // 2][at : at + 8]


def fold(c, slot, skip, sums, plain, result):
    lane = lax.broadcasted_iota(jnp.int32, (8, LANES), 1)
    for u in range(8):
        y = None
        for d in range(4):
            v = None
            for j in range(4):
                r = (j + d) % 4
                low = sums[slot, r, 8 + 8 * u - j : 16 + 8 * u - j, 0:LANES]
                high = sums[slot, r, 4 + 8 * u - j : 12 + 8 * u - j, LANES : 2 * LANES]
                w = low + high
                v = w if v is None else jnp.where(lane >= 32 * j, w, v)
            if d:
                v = pltpu.roll(v, 32 * d, 1)
            y = v if y is None else y + v
        at = pl.ds(8 * u * C + c, 8, stride=C)
        result[at, :] = y + skip * plain[at, :]


def kernel(
    gate_hbm, key_hbm, value_hbm, filter_hbm,
    gate_short, key_short, value_short, skip_gain, norm_gain,
    out,
    gate_in, key_in, value_in, filter_in, load_sem,
    gate_full, key_full, value_full,
    edge_out, edge_in, edge_send, edge_recv,
    filter_send, filter_recv, product_send, product_recv, mixed_send, mixed_recv,
    sems,
    gated, taps, plain, flipped, result, left, right, sums,
    square_send, square_recv, square_sems, turned,
    key_tail, value_tail, gate_tail, tail_sem,
):
    me, ch = lax.axis_index("seq"), lax.axis_index("ch")
    tails = [
        pltpu.make_async_copy(src.at[pl.ds(TOK - 16, 16)], dst, tail_sem.at[i])
        for i, (src, dst) in enumerate(
            ((key_hbm, key_tail), (value_hbm, value_tail), (gate_hbm, gate_tail))
        )
    ]
    loads = [
        pltpu.make_async_copy(src, dst, load_sem.at[i])
        for i, (src, dst) in enumerate(
            ((filter_hbm, filter_in), (key_hbm, key_in), (value_hbm, value_in), (gate_hbm, gate_in))
        )
    ]
    for load in tails + loads:
        load.start()

    barrier = pltpu.get_barrier_semaphore()

    peers = others(me)
    for peer in peers:
        pl.semaphore_signal(barrier, inc=1, device_id=(peer, ch), device_id_type=MESH)
    for d in range(1, GROUPS):
        pl.semaphore_signal(
            barrier, inc=1, device_id=(me, lax.rem(ch + d, GROUPS)), device_id_type=MESH
        )

    for load in tails:
        load.wait()
    edge_out[...] = jnp.zeros_like(edge_out)
    for i, tail in enumerate((key_tail, value_tail, gate_tail)):
        edge_out[2 * i : 2 * i + 2, :] = tail[...].astype(F32)[14:16]

    pl.semaphore_wait(barrier, BLOCKS - 1 + GROUPS - 1)
    edge = pltpu.make_async_remote_copy(
        src_ref=edge_out,
        dst_ref=edge_in,
        send_sem=edge_send,
        recv_sem=edge_recv,
        device_id=(lax.rem(me + 1, BLOCKS), ch),
        device_id_type=MESH,
    )
    edge.start()
    loads[0].wait()

    def cut_filter(block, carry):
        split_rows(filter_in[:, lanes_of(block)].astype(F32), block, filter_send)
        return carry

    lax.fori_loop(0, WIDTH // LANES, cut_filter, 0)
    filter_sems, product_sems, mixed_sems = (
        (sems.at[2 * i], sems.at[2 * i + 1]) for i in range(3)
    )
    exchange(me, ch, peers, filter_send, filter_recv, 0, *filter_sems)

    for load, src, full in zip(
        loads[1:], (key_in, value_in, gate_in), (key_full, value_full, gate_full)
    ):
        load.wait()
        full[8 : 8 + TOK, :] = src[...].astype(F32)
    edge.wait()
    for i, full in enumerate((key_full, value_full, gate_full)):
        full[6:8, :] = jnp.where(me == 0, 0.0, edge_in[2 * i : 2 * i + 2, :])

    def cut_product(block, carry):
        product = short_conv(key_full, key_short, block) * short_conv(
            value_full, value_short, block
        )
        split_rows(product.astype(BF).astype(F32), block, product_send)
        return carry

    lax.fori_loop(0, WIDTH // LANES, cut_product, 0)
    exchange(me, ch, peers, product_send, product_recv, 0, *product_sems)

    def exchange_both(part, carry):
        exchange(me, ch, peers, filter_send, filter_recv, part, *filter_sems)
        exchange(me, ch, peers, product_send, product_recv, part, *product_sems)
        return carry

    lax.fori_loop(1, PARTS, exchange_both, 0)

    def turn_gate(block, carry):
        gate = short_conv(gate_full, gate_short, block)
        gated[lanes_of(block), 0:LANES] = gate[:LANES].T
        gated[lanes_of(block), LANES : 2 * LANES] = gate[LANES:].T
        return carry

    lax.fori_loop(0, WIDTH // LANES, turn_gate, 0)

    taps[0:C, :] = jnp.zeros((C, LANES), F32)
    flipped[0:C, :] = jnp.zeros((C, LANES), F32)
    for slot in range(SLOTS):
        left[slot, 0:32, :] = jnp.zeros((32, LANES), BF)
        for r in range(4):
            sums[slot, r, 0:8, :] = jnp.zeros((8, 2 * LANES), F32)
    rows = lax.broadcasted_iota(jnp.int32, (LANES, LANES), 0)
    cols = lax.broadcasted_iota(jnp.int32, (LANES, LANES), 1)
    flip = jnp.where(rows + cols == LANES - 1, 1.0, 0.0).astype(BF)

    def convolve(part, carry):
        arrived(filter_recv, part, filter_sems[1])
        taps[C:, :] = filter_recv[part].astype(F32)
        arrived(product_recv, part, product_sems[1])
        plain[...] = product_recv[part].astype(F32)
        flipped[C:, :] = jnp.dot(product_recv[part], flip, preferred_element_type=F32)

        def channels(i, carry):
            for slot in range(SLOTS):
                c = i * SLOTS + slot
                make_left(c, slot, taps, left)
                make_right(c, slot, flipped, right)
                multiply(slot, left, right, sums)
                skip = skip_gain[me * (PARTS * C) + part * C + c]
                fold(c, slot, skip, sums, plain, result)
            return carry

        lax.fori_loop(0, C // SLOTS, channels, 0)
        mixed_send[part] = result[...].astype(BF)
        exchange(me, ch, peers, mixed_send, mixed_recv, part, *mixed_sems)
        return carry

    lax.fori_loop(0, PARTS, convolve, 0)

    def gate_part(part, squares):
        arrived(mixed_recv, part, mixed_sems[1])

        def gate_owner(owner, squares):
            pair = mixed_recv[part, pl.ds(pl.multiple_of(owner * 16, 16), 16), :].astype(F32)
            at = pl.ds(pl.multiple_of(owner * (PARTS * C) + part * C, C), C)
            g = gated[at, :] * jnp.concatenate([pair[:C], pair[C:]], axis=1)
            gated[at, :] = g
            return squares + g * g

        return lax.fori_loop(0, BLOCKS, gate_owner, squares, unroll=4)

    squares = lax.fori_loop(0, PARTS, gate_part, jnp.zeros((C, TOK), F32))
    square_send[...] = squares
    tells = [
        pltpu.make_async_remote_copy(
            src_ref=square_send,
            dst_ref=square_recv.at[d - 1],
            send_sem=square_sems.at[0, d - 1],
            recv_sem=square_sems.at[1, d - 1],
            device_id=(me, lax.rem(ch + d, GROUPS)),
            device_id_type=MESH,
        )
        for d in range(1, GROUPS)
    ]
    for tell in tells:
        tell.start()

    def turn_back(block, carry):
        at = lanes_of(block)
        turned[:, at] = gated[at, :].T * norm_gain[0:1, at]
        return carry

    lax.fori_loop(0, WIDTH // LANES, turn_back, 0)
    for tell in tells:
        tell.wait()
    for d in range(GROUPS - 1):
        squares = squares + square_recv[d]
    meansq = jnp.sum(squares, axis=0, keepdims=True) / (WIDTH * GROUPS)
    inverse = lax.rsqrt(meansq + 1e-06)
    scale = jnp.broadcast_to(inverse, (LANES, TOK)).T

    for block in range(WIDTH // LANES):
        at = slice(LANES * block, LANES * block + LANES)
        out[:, at] = (turned[:, at] * scale).astype(BF)

    edge_free = [(filter_send, filter_sems), (product_send, product_sems), (mixed_send, mixed_sems)]
    for src, pair in edge_free:
        for part in range(PARTS):
            sent(src, part, pair[0])


def local(
    gate_in, key_in, value_in, long_filter, gate_short, key_short, value_short, skip_gain, norm_gain
):
    vmem = pl.BlockSpec(memory_space=pltpu.VMEM)
    smem = pl.BlockSpec(memory_space=pltpu.SMEM)
    hbm = pl.BlockSpec(memory_space=pl.ANY)
    parts = (PARTS, ROWS, LANES)
    return pl.pallas_call(
        kernel,
        out_shape=jax.ShapeDtypeStruct((TOK, WIDTH), BF),
        in_specs=[hbm] * 4 + [vmem] * 3 + [smem, vmem],
        out_specs=vmem,
        scratch_shapes=[
            *[pltpu.VMEM((TOK, WIDTH), BF)] * 4,
            pltpu.SemaphoreType.DMA((4,)),
            *[pltpu.VMEM((8 + TOK, WIDTH), F32)] * 3,
            *[pltpu.VMEM((8, WIDTH), F32)] * 2,
            pltpu.SemaphoreType.DMA,
            pltpu.SemaphoreType.DMA,
            *[pltpu.VMEM(parts, BF)] * 6,
            pltpu.SemaphoreType.DMA((6, PARTS)),
            pltpu.VMEM((WIDTH, TOK), F32),
            pltpu.VMEM((ROWS + C, LANES), F32),
            pltpu.VMEM((ROWS, LANES), F32),
            pltpu.VMEM((ROWS + C, LANES), F32),
            pltpu.VMEM((ROWS, LANES), F32),
            pltpu.VMEM((SLOTS, 288, LANES), BF),
            pltpu.VMEM((SLOTS, 4, 256, 256), BF),
            pltpu.VMEM((SLOTS, 4, 72, 256), F32),
            pltpu.VMEM((C, TOK), F32),
            pltpu.VMEM((GROUPS - 1, C, TOK), F32),
            pltpu.SemaphoreType.DMA((2, GROUPS - 1)),
            pltpu.VMEM((TOK, WIDTH), F32),
            *[pltpu.VMEM((16, WIDTH), BF)] * 3,
            pltpu.SemaphoreType.DMA((3,)),
        ],
        compiler_params=pltpu.CompilerParams(
            collective_id=0, has_side_effects=True, vmem_limit_bytes=60 << 20
        ),
        name="hyena",
    )(
        gate_in, key_in, value_in, long_filter,
        gate_short, key_short, value_short, skip_gain, norm_gain.reshape(1, WIDTH),
    )


def solution(mesh):
    return jax.shard_map(
        local,
        mesh=mesh,
        in_specs=(
            P("seq", "ch"),
            P("seq", "ch"),
            P("seq", "ch"),
            P("seq", "ch"),
            P(None, "ch"),
            P(None, "ch"),
            P(None, "ch"),
            P("ch"),
            P("ch"),
        ),
        out_specs=P("seq", "ch"),
        check_vma=False,
    )
```

```python
import functools

import jax
import jax.numpy as jnp
from jax import lax
from jax.experimental import pallas as pl
from jax.experimental.pallas import tpu as pltpu
from jax.sharding import PartitionSpec as P

MESH = pl.DeviceIdType.MESH
F32, BF = jnp.float32, jnp.bfloat16
NT = (((1,), (1,)), ((), ()))

BLOCKS = 32
GROUPS = 4
TOK = 256
WIDTH = 1024
PARTS = 4
C = 8
SLOTS = 4
LANES = 128
STAGES = (2, 1, 0)
SEGS = 64
ROWS = SEGS * C


def others(me):
    ys = [lax.rem(me // 8 + d, 4) * 8 for d in range(4)]
    zs = [lax.rem(me // 2 + d, 4) * 2 for d in range(4)]
    cores = [lax.rem(me + d, 2) for d in range(2)]
    return [y + z + core for y in ys for z in zs for core in cores][1:]


def exchange(me, ch, peers, src, dst, part, send_sem, recv_sem):
    mine = pl.ds(pl.multiple_of(me * 16, 16), 16)
    pltpu.make_async_copy(src.at[part, mine], dst.at[part, mine], recv_sem.at[part]).start()
    for peer in peers:
        pltpu.make_async_remote_copy(
            src_ref=src.at[part, pl.ds(pl.multiple_of(peer * 16, 16), 16)],
            dst_ref=dst.at[part, mine],
            send_sem=send_sem.at[part],
            recv_sem=recv_sem.at[part],
            device_id=(peer, ch),
            device_id_type=MESH,
        ).start()


def arrived(dst, part, recv_sem):
    pltpu.make_async_copy(dst.at[part], dst.at[part], recv_sem.at[part]).wait()


def sent(src, part, send_sem):
    piece = src.at[part, pl.ds(0, 16 * (BLOCKS - 1))]
    pltpu.make_async_copy(piece, piece, send_sem.at[part]).wait()


def lanes_of(block):
    return pl.ds(pl.multiple_of(block * LANES, LANES), LANES)


def short_conv(full, taps, block):
    at = lanes_of(block)
    return (
        taps[0:1, at] * full[8 : 8 + TOK, at]
        + taps[1:2, at] * full[7 : 7 + TOK, at]
        + taps[2:3, at] * full[6 : 6 + TOK, at]
    )


def split_rows(tokens, block, dst):
    first, second = tokens[:LANES].T, tokens[LANES:].T
    for group in range(LANES // C):
        rows = slice(C * group, C * group + C)
        pair = jnp.concatenate([first[rows], second[rows]], axis=0).astype(BF)
        owner = block * 4 + group // PARTS
        dst[group % PARTS, pl.ds(pl.multiple_of(owner * 16, 16), 16), :] = pair


def make_left(c, slot, taps, left):
    lane = lax.broadcasted_iota(jnp.int32, (8, LANES), 1)
    for u in range(8):
        here = taps[pl.ds((1 + 8 * u) * C + c, 8, stride=C), :]
        before = taps[pl.ds(8 * u * C + c, 8, stride=C), :]
        phases = []
        for r in range(4):
            by = 32 * (3 - r)
            if by:
                phases.append(pltpu.roll(jnp.where(lane >= LANES - by, before, here), by, 1))
            else:
                phases.append(here)
        left[slot, 32 + 32 * u : 64 + 32 * u, :] = jnp.concatenate(phases, axis=0).astype(BF)
        if u % 2:
            yield


def make_right(c, slot, flipped, right):
    lane = lax.broadcasted_iota(jnp.int32, (8, LANES), 1)
    row = lax.broadcasted_iota(jnp.int32, (8, LANES), 0)
    masks = [lane < 31 - 8 * o - row for o in range(4)]
    before = jnp.broadcast_to(flipped[pl.ds(c, 1), :], (8, LANES))
    for m in range(SEGS):
        b, g = m // 8, m % 8
        here = jnp.broadcast_to(flipped[pl.ds((m + 1) * C + c, 1), :], (8, LANES))
        phases = [
            pltpu.roll(
                jnp.where(masks[o], before, here), 97 + 8 * o, 1, stride=1, stride_axis=0
            )
            for o in range(4)
        ]
        half = LANES * (b % 2)
        right[slot, b // 2, 32 * g : 32 * g + 32, half : half + LANES] = jnp.concatenate(
            phases, axis=0
        ).astype(BF)
        before = here
        if m % 16 == 15:
            yield


def multiply(slot, left, right, sums):
    total = None
    for k in range(4):
        n = 256 - 64 * k
        lhs = jnp.concatenate([left[slot, 32 : 32 + n, :], left[slot, 0:n, :]], axis=1)
        part = lax.dot_general(lhs, right[slot, k], NT, preferred_element_type=F32)
        if total is None:
            total = [part[64 * i : 64 * i + 64] for i in range(4)]
        else:
            for i in range(k, 4):
                total[i] = total[i] + part[64 * (i - k) : 64 * (i - k) + 64]
        if k < 3:
            yield
    for u in range(8):
        for r in range(4):
            at = 32 * (u % 2) + 8 * r
            sums[slot, r, 12 + 8 * u : 20 + 8 * u, LANES:] = total[u // 2][at : at + 8, LANES:]
    for u in range(8):
        for r in range(4):
            at = 32 * (u % 2) + 8 * r
            rows = slice(8 + 8 * u, 16 + 8 * u)
            sums[slot, r, rows, 0:LANES] = (
                total[u // 2][at : at + 8, 0:LANES] + sums[slot, r, rows, LANES:]
            )
    yield


def fold(c, slot, skip, sums, plain, result):
    lane = lax.broadcasted_iota(jnp.int32, (8, LANES), 1)
    for u in range(8):
        y = None
        for d in range(4):
            v = None
            for j in range(4):
                r = (j + d) % 4
                w = sums[slot, r, 8 + 8 * u - j : 16 + 8 * u - j, 0:LANES]
                v = w if v is None else jnp.where(lane >= 32 * j, w, v)
            if d:
                v = pltpu.roll(v, 32 * d, 1)
            y = v if y is None else y + v
        at = pl.ds(8 * u * C + c, 8, stride=C)
        result[at, :] = y + skip * plain[at, :]
        if u % 2:
            yield


def kernel(
    gate_hbm, key_hbm, value_hbm, filter_hbm,
    gate_short, key_short, value_short, skip_gain, norm_gain,
    out,
    gate_in, key_in, value_in, filter_in, load_sem,
    gate_full, key_full, value_full,
    edge_out, edge_in, edge_send, edge_recv,
    filter_send, filter_recv, product_send, product_recv, mixed_send, mixed_recv,
    sems,
    gated, taps, plain, flipped, result, left, right, sums,
    square_send, square_recv, square_sems, turned,
    key_tail, value_tail, gate_tail, tail_sem,
):
    me, ch = lax.axis_index("seq"), lax.axis_index("ch")
    tails = [
        pltpu.make_async_copy(src.at[pl.ds(TOK - 16, 16)], dst, tail_sem.at[i])
        for i, (src, dst) in enumerate(
            ((key_hbm, key_tail), (value_hbm, value_tail), (gate_hbm, gate_tail))
        )
    ]
    loads = [
        pltpu.make_async_copy(src, dst, load_sem.at[i])
        for i, (src, dst) in enumerate(
            ((filter_hbm, filter_in), (key_hbm, key_in), (value_hbm, value_in), (gate_hbm, gate_in))
        )
    ]
    for load in tails + loads:
        load.start()

    barrier = pltpu.get_barrier_semaphore()

    peers = others(me)
    for peer in peers:
        pl.semaphore_signal(barrier, inc=1, device_id=(peer, ch), device_id_type=MESH)
    for d in range(1, GROUPS):
        pl.semaphore_signal(
            barrier, inc=1, device_id=(me, lax.rem(ch + d, GROUPS)), device_id_type=MESH
        )

    for load in tails:
        load.wait()
    edge_out[...] = jnp.zeros_like(edge_out)
    for i, tail in enumerate((key_tail, value_tail, gate_tail)):
        edge_out[2 * i : 2 * i + 2, :] = tail[...].astype(F32)[14:16]

    pl.semaphore_wait(barrier, BLOCKS - 1 + GROUPS - 1)
    edge = pltpu.make_async_remote_copy(
        src_ref=edge_out,
        dst_ref=edge_in,
        send_sem=edge_send,
        recv_sem=edge_recv,
        device_id=(lax.rem(me + 1, BLOCKS), ch),
        device_id_type=MESH,
    )
    edge.start()
    loads[0].wait()

    def cut_filter(block, carry):
        split_rows(filter_in[:, lanes_of(block)].astype(F32), block, filter_send)
        return carry

    lax.fori_loop(0, WIDTH // LANES, cut_filter, 0)
    filter_sems, product_sems, mixed_sems = (
        (sems.at[2 * i], sems.at[2 * i + 1]) for i in range(3)
    )
    exchange(me, ch, peers, filter_send, filter_recv, 0, *filter_sems)

    for load, src, full in zip(
        loads[1:], (key_in, value_in, gate_in), (key_full, value_full, gate_full)
    ):
        load.wait()
        full[8 : 8 + TOK, :] = src[...].astype(F32)
    edge.wait()
    for i, full in enumerate((key_full, value_full, gate_full)):
        full[6:8, :] = jnp.where(me == 0, 0.0, edge_in[2 * i : 2 * i + 2, :])

    def cut_product(block, carry):
        product = short_conv(key_full, key_short, block) * short_conv(
            value_full, value_short, block
        )
        split_rows(product.astype(BF).astype(F32), block, product_send)
        return carry

    lax.fori_loop(0, WIDTH // LANES, cut_product, 0)
    exchange(me, ch, peers, product_send, product_recv, 0, *product_sems)

    def exchange_both(part, carry):
        exchange(me, ch, peers, filter_send, filter_recv, part, *filter_sems)
        exchange(me, ch, peers, product_send, product_recv, part, *product_sems)
        return carry


    def turn_gate(block, carry):
        gate = short_conv(gate_full, gate_short, block)
        gated[lanes_of(block), 0:LANES] = gate[:LANES].T
        gated[lanes_of(block), LANES : 2 * LANES] = gate[LANES:].T
        return carry

    lax.fori_loop(0, WIDTH // LANES, turn_gate, 0)
    lax.fori_loop(1, PARTS, exchange_both, 0)

    taps[0:C, :] = jnp.zeros((C, LANES), F32)
    flipped[0:C, :] = jnp.zeros((C, LANES), F32)
    for slot in range(SLOTS):
        left[slot, 0:32, :] = jnp.zeros((32, LANES), BF)
        for r in range(4):
            sums[slot, r, 0:16, :] = jnp.zeros((16, 2 * LANES), F32)
    rows = lax.broadcasted_iota(jnp.int32, (LANES, LANES), 0)
    cols = lax.broadcasted_iota(jnp.int32, (LANES, LANES), 1)
    flip = jnp.where(rows + cols == LANES - 1, 1.0, 0.0).astype(BF)

    def convolve(part, carry):
        arrived(filter_recv, part, filter_sems[1])
        taps[C:, :] = filter_recv[part].astype(F32)
        arrived(product_recv, part, product_sems[1])
        plain[...] = product_recv[part].astype(F32)
        flipped[C:, :] = jnp.dot(product_recv[part], flip, preferred_element_type=F32)

        def channels(i, carry):
            work = []
            for slot in range(SLOTS):
                c = i * SLOTS + slot
                skip = skip_gain[me * (PARTS * C) + part * C + c]
                work.append(
                    (
                        (make_left(c, slot, taps, left), make_right(c, slot, flipped, right)),
                        (multiply(slot, left, right, sums),),
                        (fold(c, slot, skip, sums, plain, result),),
                    )
                )
            for beat in range(SLOTS + 2):
                turns = [
                    steps
                    for stage in STAGES
                    if 0 <= beat - stage < SLOTS
                    for steps in work[beat - stage][stage]
                ]
                for _ in range(4):
                    for steps in turns:
                        next(steps, None)
            return carry

        lax.fori_loop(0, C // SLOTS, channels, 0)
        mixed_send[part] = result[...].astype(BF)
        exchange(me, ch, peers, mixed_send, mixed_recv, part, *mixed_sems)
        return carry

    lax.fori_loop(0, PARTS, convolve, 0)

    def gate_part(part, squares):
        arrived(mixed_recv, part, mixed_sems[1])

        def gate_owner(owner, squares):
            pair = mixed_recv[part, pl.ds(pl.multiple_of(owner * 16, 16), 16), :].astype(F32)
            at = pl.ds(pl.multiple_of(owner * (PARTS * C) + part * C, C), C)
            g = gated[at, :] * jnp.concatenate([pair[:C], pair[C:]], axis=1)
            gated[at, :] = g
            return squares + g * g

        return lax.fori_loop(0, BLOCKS, gate_owner, squares, unroll=4)

    squares = lax.fori_loop(0, PARTS, gate_part, jnp.zeros((C, TOK), F32))
    square_send[...] = squares
    tells = [
        pltpu.make_async_remote_copy(
            src_ref=square_send,
            dst_ref=square_recv.at[d - 1],
            send_sem=square_sems.at[0, d - 1],
            recv_sem=square_sems.at[1, d - 1],
            device_id=(me, lax.rem(ch + d, GROUPS)),
            device_id_type=MESH,
        )
        for d in range(1, GROUPS)
    ]
    for tell in tells:
        tell.start()

    def turn_back(block, carry):
        at = lanes_of(block)
        turned[:, at] = gated[at, :].T * norm_gain[0:1, at]
        return carry

    lax.fori_loop(0, WIDTH // LANES, turn_back, 0)
    for tell in tells:
        tell.wait()
    for d in range(GROUPS - 1):
        squares = squares + square_recv[d]
    meansq = jnp.sum(squares, axis=0, keepdims=True) / (WIDTH * GROUPS)
    inverse = lax.rsqrt(meansq + 1e-06)
    scale = jnp.broadcast_to(inverse, (LANES, TOK)).T

    for block in range(WIDTH // LANES):
        at = slice(LANES * block, LANES * block + LANES)
        out[:, at] = (turned[:, at] * scale).astype(BF)

    edge_free = [(filter_send, filter_sems), (product_send, product_sems), (mixed_send, mixed_sems)]
    for src, pair in edge_free:
        for part in range(PARTS):
            sent(src, part, pair[0])


def local(
    gate_in, key_in, value_in, long_filter, gate_short, key_short, value_short, skip_gain, norm_gain
):
    vmem = pl.BlockSpec(memory_space=pltpu.VMEM)
    smem = pl.BlockSpec(memory_space=pltpu.SMEM)
    hbm = pl.BlockSpec(memory_space=pl.ANY)
    parts = (PARTS, ROWS, LANES)
    return pl.pallas_call(
        kernel,
        out_shape=jax.ShapeDtypeStruct((TOK, WIDTH), BF),
        in_specs=[hbm] * 4 + [vmem] * 3 + [smem, vmem],
        out_specs=vmem,
        scratch_shapes=[
            *[pltpu.VMEM((TOK, WIDTH), BF)] * 4,
            pltpu.SemaphoreType.DMA((4,)),
            *[pltpu.VMEM((8 + TOK, WIDTH), F32)] * 3,
            *[pltpu.VMEM((8, WIDTH), F32)] * 2,
            pltpu.SemaphoreType.DMA,
            pltpu.SemaphoreType.DMA,
            *[pltpu.VMEM(parts, BF)] * 6,
            pltpu.SemaphoreType.DMA((6, PARTS)),
            pltpu.VMEM((WIDTH, TOK), F32),
            pltpu.VMEM((ROWS + C, LANES), F32),
            pltpu.VMEM((ROWS, LANES), F32),
            pltpu.VMEM((ROWS + C, LANES), F32),
            pltpu.VMEM((ROWS, LANES), F32),
            pltpu.VMEM((SLOTS, 288, LANES), BF),
            pltpu.VMEM((SLOTS, 4, 256, 256), BF),
            pltpu.VMEM((SLOTS, 4, 80, 256), F32),
            pltpu.VMEM((C, TOK), F32),
            pltpu.VMEM((GROUPS - 1, C, TOK), F32),
            pltpu.SemaphoreType.DMA((2, GROUPS - 1)),
            pltpu.VMEM((TOK, WIDTH), F32),
            *[pltpu.VMEM((16, WIDTH), BF)] * 3,
            pltpu.SemaphoreType.DMA((3,)),
        ],
        compiler_params=pltpu.CompilerParams(
            collective_id=0, has_side_effects=True, vmem_limit_bytes=60 << 20
        ),
        name="hyena",
    )(
        gate_in, key_in, value_in, long_filter,
        gate_short, key_short, value_short, skip_gain, norm_gain.reshape(1, WIDTH),
    )


def solution(mesh):
    return jax.shard_map(
        local,
        mesh=mesh,
        in_specs=(
            P("seq", "ch"),
            P("seq", "ch"),
            P("seq", "ch"),
            P("seq", "ch"),
            P(None, "ch"),
            P(None, "ch"),
            P(None, "ch"),
            P("ch"),
            P("ch"),
        ),
        out_specs=P("seq", "ch"),
        check_vma=False,
    )
```

```python
import functools

import jax
import jax.numpy as jnp
from jax import lax
from jax.experimental import pallas as pl
from jax.experimental.pallas import tpu as pltpu
from jax.sharding import PartitionSpec as P

MESH = pl.DeviceIdType.MESH
F32, BF = jnp.float32, jnp.bfloat16
NT = (((1,), (1,)), ((), ()))

BLOCKS = 32
GROUPS = 4
TOK = 256
WIDTH = 1024
PARTS = 4
C = 8
SLOTS = 4
LANES = 128
STAGES = (2, 1, 0)
SEGS = 64
ROWS = SEGS * C


def others(me):
    ys = [lax.rem(me // 8 + d, 4) * 8 for d in range(4)]
    zs = [lax.rem(me // 2 + d, 4) * 2 for d in range(4)]
    cores = [lax.rem(me + d, 2) for d in range(2)]
    return [y + z + core for y in ys for z in zs for core in cores][1:]


def exchange(me, ch, peers, src, dst, part, send_sem, recv_sem):
    mine = pl.ds(pl.multiple_of(me * 16, 16), 16)
    pltpu.make_async_copy(src.at[part, mine], dst.at[part, mine], recv_sem.at[part]).start()
    for peer in peers:
        pltpu.make_async_remote_copy(
            src_ref=src.at[part, pl.ds(pl.multiple_of(peer * 16, 16), 16)],
            dst_ref=dst.at[part, mine],
            send_sem=send_sem.at[part],
            recv_sem=recv_sem.at[part],
            device_id=(peer, ch),
            device_id_type=MESH,
        ).start()


def arrived(dst, part, recv_sem):
    pltpu.make_async_copy(dst.at[part], dst.at[part], recv_sem.at[part]).wait()


def sent(src, part, send_sem):
    piece = src.at[part, pl.ds(0, 16 * (BLOCKS - 1))]
    pltpu.make_async_copy(piece, piece, send_sem.at[part]).wait()


def lanes_of(block):
    return pl.ds(pl.multiple_of(block * LANES, LANES), LANES)


def short_conv(full, taps, block):
    at = lanes_of(block)
    return (
        taps[0:1, at] * full[8 : 8 + TOK, at]
        + taps[1:2, at] * full[7 : 7 + TOK, at]
        + taps[2:3, at] * full[6 : 6 + TOK, at]
    )


def split_rows(tokens, block, dst):
    first, second = tokens[:LANES].T, tokens[LANES:].T
    for group in range(LANES // C):
        rows = slice(C * group, C * group + C)
        pair = jnp.concatenate([first[rows], second[rows]], axis=0).astype(BF)
        owner = lax.rem(block, 2) * (LANES // C) + group
        dst[block // 2, pl.ds(pl.multiple_of(owner * 16, 16), 16), :] = pair


def make_left(c, slot, taps, left):
    lane = lax.broadcasted_iota(jnp.int32, (8, LANES), 1)
    for u in range(8):
        here = taps[pl.ds((1 + 8 * u) * C + c, 8, stride=C), :]
        before = taps[pl.ds(8 * u * C + c, 8, stride=C), :]
        phases = []
        for r in range(4):
            by = 32 * (3 - r)
            if by:
                phases.append(pltpu.roll(jnp.where(lane >= LANES - by, before, here), by, 1))
            else:
                phases.append(here)
        left[slot, 32 + 32 * u : 64 + 32 * u, :] = jnp.concatenate(phases, axis=0).astype(BF)
        if u % 2:
            yield


def make_right(c, slot, flipped, right):
    lane = lax.broadcasted_iota(jnp.int32, (8, LANES), 1)
    row = lax.broadcasted_iota(jnp.int32, (8, LANES), 0)
    masks = [lane < 31 - 8 * o - row for o in range(4)]
    before = jnp.broadcast_to(flipped[pl.ds(c, 1), :], (8, LANES))
    for m in range(SEGS):
        b, g = m // 8, m % 8
        here = jnp.broadcast_to(flipped[pl.ds((m + 1) * C + c, 1), :], (8, LANES))
        phases = [
            pltpu.roll(
                jnp.where(masks[o], before, here), 97 + 8 * o, 1, stride=1, stride_axis=0
            )
            for o in range(4)
        ]
        half = LANES * (b % 2)
        right[slot, b // 2, 32 * g : 32 * g + 32, half : half + LANES] = jnp.concatenate(
            phases, axis=0
        ).astype(BF)
        before = here
        if m % 16 == 15:
            yield


def multiply(slot, left, right, sums):
    total = None
    for k in range(4):
        n = 256 - 64 * k
        lhs = jnp.concatenate([left[slot, 32 : 32 + n, :], left[slot, 0:n, :]], axis=1)
        part = lax.dot_general(lhs, right[slot, k], NT, preferred_element_type=F32)
        if total is None:
            total = [part[64 * i : 64 * i + 64] for i in range(4)]
        else:
            for i in range(k, 4):
                total[i] = total[i] + part[64 * (i - k) : 64 * (i - k) + 64]
        if k < 3:
            yield
    for u in range(8):
        for r in range(4):
            at = 32 * (u % 2) + 8 * r
            sums[slot, r, 12 + 8 * u : 20 + 8 * u, LANES:] = total[u // 2][at : at + 8, LANES:]
    for u in range(8):
        for r in range(4):
            at = 32 * (u % 2) + 8 * r
            rows = slice(8 + 8 * u, 16 + 8 * u)
            sums[slot, r, rows, 0:LANES] = (
                total[u // 2][at : at + 8, 0:LANES] + sums[slot, r, rows, LANES:]
            )
    yield


def fold(c, slot, skip, sums, plain, result):
    lane = lax.broadcasted_iota(jnp.int32, (8, LANES), 1)
    for u in range(8):
        y = None
        for d in range(4):
            v = None
            for j in range(4):
                r = (j + d) % 4
                w = sums[slot, r, 8 + 8 * u - j : 16 + 8 * u - j, 0:LANES]
                v = w if v is None else jnp.where(lane >= 32 * j, w, v)
            if d:
                v = pltpu.roll(v, 32 * d, 1)
            y = v if y is None else y + v
        at = pl.ds(8 * u * C + c, 8, stride=C)
        result[at, :] = y + skip * plain[at, :]
        if u % 2:
            yield


def kernel(
    gate_hbm, key_hbm, value_hbm, filter_hbm,
    gate_short, key_short, value_short, skip_gain, norm_gain,
    out,
    gate_in, key_in, value_in, filter_in, load_sem,
    gate_full, key_full, value_full,
    edge_out, edge_in, edge_send, edge_recv,
    filter_send, filter_recv, product_send, product_recv, mixed_send, mixed_recv,
    sems,
    gated, taps, plain, flipped, result, left, right, sums,
    square_send, square_recv, square_sems, turned,
    key_tail, value_tail, gate_tail, tail_sem,
):
    me, ch = lax.axis_index("seq"), lax.axis_index("ch")
    tails = [
        pltpu.make_async_copy(src.at[pl.ds(TOK - 16, 16)], dst, tail_sem.at[i])
        for i, (src, dst) in enumerate(
            ((key_hbm, key_tail), (value_hbm, value_tail), (gate_hbm, gate_tail))
        )
    ]
    loads = [
        pltpu.make_async_copy(src, dst, load_sem.at[i])
        for i, (src, dst) in enumerate(
            ((filter_hbm, filter_in), (key_hbm, key_in), (value_hbm, value_in), (gate_hbm, gate_in))
        )
    ]
    for load in tails + loads:
        load.start()

    barrier = pltpu.get_barrier_semaphore()

    peers = others(me)
    for peer in peers:
        pl.semaphore_signal(barrier, inc=1, device_id=(peer, ch), device_id_type=MESH)
    for d in range(1, GROUPS):
        pl.semaphore_signal(
            barrier, inc=1, device_id=(me, lax.rem(ch + d, GROUPS)), device_id_type=MESH
        )

    for load in tails:
        load.wait()
    edge_out[...] = jnp.zeros_like(edge_out)
    for i, tail in enumerate((key_tail, value_tail, gate_tail)):
        edge_out[2 * i : 2 * i + 2, :] = tail[...].astype(F32)[14:16]

    pl.semaphore_wait(barrier, BLOCKS - 1 + GROUPS - 1)
    edge = pltpu.make_async_remote_copy(
        src_ref=edge_out,
        dst_ref=edge_in,
        send_sem=edge_send,
        recv_sem=edge_recv,
        device_id=(lax.rem(me + 1, BLOCKS), ch),
        device_id_type=MESH,
    )
    edge.start()
    loads[0].wait()

    def cut_filter(block, carry):
        split_rows(filter_in[:, lanes_of(block)].astype(F32), block, filter_send)
        return carry

    filter_sems, product_sems, mixed_sems = (
        (sems.at[2 * i], sems.at[2 * i + 1]) for i in range(3)
    )
    lax.fori_loop(0, 2, cut_filter, 0)
    exchange(me, ch, peers, filter_send, filter_recv, 0, *filter_sems)

    for load in loads[1:]:
        load.wait()
    edge.wait()
    for i, full in enumerate((key_full, value_full, gate_full)):
        full[6:8, :] = jnp.where(me == 0, 0.0, edge_in[2 * i : 2 * i + 2, :])

    def cut_product(block, carry):
        at = lanes_of(block)
        key_full[8 : 8 + TOK, at] = key_in[:, at].astype(F32)
        value_full[8 : 8 + TOK, at] = value_in[:, at].astype(F32)
        product = short_conv(key_full, key_short, block) * short_conv(
            value_full, value_short, block
        )
        split_rows(product.astype(BF).astype(F32), block, product_send)
        return carry

    lax.fori_loop(0, 2, cut_product, 0)
    exchange(me, ch, peers, product_send, product_recv, 0, *product_sems)

    def exchange_both(part, carry):
        lax.fori_loop(2 * part, 2 * part + 2, cut_filter, 0)
        exchange(me, ch, peers, filter_send, filter_recv, part, *filter_sems)
        lax.fori_loop(2 * part, 2 * part + 2, cut_product, 0)
        exchange(me, ch, peers, product_send, product_recv, part, *product_sems)
        return carry

    def turn_gate(block, carry):
        at = lanes_of(block)
        gate_full[8 : 8 + TOK, at] = gate_in[:, at].astype(F32)
        gate = short_conv(gate_full, gate_short, block)
        gated[lanes_of(block), 0:LANES] = gate[:LANES].T
        gated[lanes_of(block), LANES : 2 * LANES] = gate[LANES:].T
        return carry

    lax.fori_loop(1, PARTS, exchange_both, 0)

    taps[0:C, :] = jnp.zeros((C, LANES), F32)
    flipped[0:C, :] = jnp.zeros((C, LANES), F32)
    for slot in range(SLOTS):
        left[slot, 0:32, :] = jnp.zeros((32, LANES), BF)
        for r in range(4):
            sums[slot, r, 0:16, :] = jnp.zeros((16, 2 * LANES), F32)
    rows = lax.broadcasted_iota(jnp.int32, (LANES, LANES), 0)
    cols = lax.broadcasted_iota(jnp.int32, (LANES, LANES), 1)
    flip = jnp.where(rows + cols == LANES - 1, 1.0, 0.0).astype(BF)

    def convolve(part, carry):
        arrived(filter_recv, part, filter_sems[1])
        taps[C:, :] = filter_recv[part].astype(F32)
        arrived(product_recv, part, product_sems[1])
        plain[...] = product_recv[part].astype(F32)
        flipped[C:, :] = jnp.dot(product_recv[part], flip, preferred_element_type=F32)

        def channels(i, carry):
            work = []
            for slot in range(SLOTS):
                c = i * SLOTS + slot
                skip = skip_gain[part * (BLOCKS * C) + me * C + c]
                work.append(
                    (
                        (make_left(c, slot, taps, left), make_right(c, slot, flipped, right)),
                        (multiply(slot, left, right, sums),),
                        (fold(c, slot, skip, sums, plain, result),),
                    )
                )
            for beat in range(SLOTS + 2):
                turns = [
                    steps
                    for stage in STAGES
                    if 0 <= beat - stage < SLOTS
                    for steps in work[beat - stage][stage]
                ]
                for _ in range(4):
                    for steps in turns:
                        next(steps, None)
            return carry

        lax.fori_loop(0, C // SLOTS, channels, 0)
        mixed_send[part] = result[...].astype(BF)
        exchange(me, ch, peers, mixed_send, mixed_recv, part, *mixed_sems)
        return carry

    lax.fori_loop(0, PARTS, convolve, 0)
    lax.fori_loop(0, WIDTH // LANES, turn_gate, 0)

    def gate_part(part, squares):
        arrived(mixed_recv, part, mixed_sems[1])

        def gate_owner(owner, squares):
            pair = mixed_recv[part, pl.ds(pl.multiple_of(owner * 16, 16), 16), :].astype(F32)
            at = pl.ds(pl.multiple_of(part * (BLOCKS * C) + owner * C, C), C)
            g = gated[at, :] * jnp.concatenate([pair[:C], pair[C:]], axis=1)
            gated[at, :] = g
            return squares + g * g

        return lax.fori_loop(0, BLOCKS, gate_owner, squares, unroll=4)

    squares = lax.fori_loop(0, PARTS, gate_part, jnp.zeros((C, TOK), F32))
    square_send[...] = squares
    tells = [
        pltpu.make_async_remote_copy(
            src_ref=square_send,
            dst_ref=square_recv.at[d - 1],
            send_sem=square_sems.at[0, d - 1],
            recv_sem=square_sems.at[1, d - 1],
            device_id=(me, lax.rem(ch + d, GROUPS)),
            device_id_type=MESH,
        )
        for d in range(1, GROUPS)
    ]
    for tell in tells:
        tell.start()

    def turn_back(block, carry):
        at = lanes_of(block)
        turned[:, at] = gated[at, :].T * norm_gain[0:1, at]
        return carry

    lax.fori_loop(0, WIDTH // LANES, turn_back, 0)
    for tell in tells:
        tell.wait()
    for d in range(GROUPS - 1):
        squares = squares + square_recv[d]
    meansq = jnp.sum(squares, axis=0, keepdims=True) / (WIDTH * GROUPS)
    inverse = lax.rsqrt(meansq + 1e-06)
    scale = jnp.broadcast_to(inverse, (LANES, TOK)).T

    for block in range(WIDTH // LANES):
        at = slice(LANES * block, LANES * block + LANES)
        out[:, at] = (turned[:, at] * scale).astype(BF)

    edge_free = [(filter_send, filter_sems), (product_send, product_sems), (mixed_send, mixed_sems)]
    for src, pair in edge_free:
        for part in range(PARTS):
            sent(src, part, pair[0])


def local(
    gate_in, key_in, value_in, long_filter, gate_short, key_short, value_short, skip_gain, norm_gain
):
    vmem = pl.BlockSpec(memory_space=pltpu.VMEM)
    smem = pl.BlockSpec(memory_space=pltpu.SMEM)
    hbm = pl.BlockSpec(memory_space=pl.ANY)
    parts = (PARTS, ROWS, LANES)
    return pl.pallas_call(
        kernel,
        out_shape=jax.ShapeDtypeStruct((TOK, WIDTH), BF),
        in_specs=[hbm] * 4 + [vmem] * 3 + [smem, vmem],
        out_specs=vmem,
        scratch_shapes=[
            *[pltpu.VMEM((TOK, WIDTH), BF)] * 4,
            pltpu.SemaphoreType.DMA((4,)),
            *[pltpu.VMEM((8 + TOK, WIDTH), F32)] * 3,
            *[pltpu.VMEM((8, WIDTH), F32)] * 2,
            pltpu.SemaphoreType.DMA,
            pltpu.SemaphoreType.DMA,
            *[pltpu.VMEM(parts, BF)] * 6,
            pltpu.SemaphoreType.DMA((6, PARTS)),
            pltpu.VMEM((WIDTH, TOK), F32),
            pltpu.VMEM((ROWS + C, LANES), F32),
            pltpu.VMEM((ROWS, LANES), F32),
            pltpu.VMEM((ROWS + C, LANES), F32),
            pltpu.VMEM((ROWS, LANES), F32),
            pltpu.VMEM((SLOTS, 288, LANES), BF),
            pltpu.VMEM((SLOTS, 4, 256, 256), BF),
            pltpu.VMEM((SLOTS, 4, 80, 256), F32),
            pltpu.VMEM((C, TOK), F32),
            pltpu.VMEM((GROUPS - 1, C, TOK), F32),
            pltpu.SemaphoreType.DMA((2, GROUPS - 1)),
            pltpu.VMEM((TOK, WIDTH), F32),
            *[pltpu.VMEM((16, WIDTH), BF)] * 3,
            pltpu.SemaphoreType.DMA((3,)),
        ],
        compiler_params=pltpu.CompilerParams(
            collective_id=0, has_side_effects=True, vmem_limit_bytes=60 << 20
        ),
        name="hyena",
    )(
        gate_in, key_in, value_in, long_filter,
        gate_short, key_short, value_short, skip_gain, norm_gain.reshape(1, WIDTH),
    )


def solution(mesh):
    return jax.shard_map(
        local,
        mesh=mesh,
        in_specs=(
            P("seq", "ch"),
            P("seq", "ch"),
            P("seq", "ch"),
            P("seq", "ch"),
            P(None, "ch"),
            P(None, "ch"),
            P(None, "ch"),
            P("ch"),
            P("ch"),
        ),
        out_specs=P("seq", "ch"),
        check_vma=False,
    )
```

```python
import functools

import jax
import jax.numpy as jnp
from jax import lax
from jax.experimental import pallas as pl
from jax.experimental.pallas import tpu as pltpu
from jax.sharding import PartitionSpec as P

MESH = pl.DeviceIdType.MESH
F32, BF = jnp.float32, jnp.bfloat16
NT = (((1,), (1,)), ((), ()))

BLOCKS = 32
GROUPS = 4
TOK = 256
WIDTH = 1024
PARTS = 4
C = 8
SLOTS = 4
LANES = 128
STAGES = (2, 1, 0)
SEGS = 64
ROWS = SEGS * C


def others(me):
    ys = [lax.rem(me // 8 + d, 4) * 8 for d in range(4)]
    zs = [lax.rem(me // 2 + d, 4) * 2 for d in range(4)]
    cores = [lax.rem(me + d, 2) for d in range(2)]
    near = (0, 1, 2, 1)
    order = sorted(
        ((dy, dz, dc) for dy in range(4) for dz in range(4) for dc in range(2)),
        key=lambda d: -near[d[0]] - near[d[1]],
    )
    return [ys[dy] + zs[dz] + cores[dc] for dy, dz, dc in order if dy + dz + dc]


def exchange(me, ch, peers, src, dst, part, send_sem, recv_sem):
    mine = pl.ds(pl.multiple_of(me * 16, 16), 16)
    pltpu.make_async_copy(src.at[part, mine], dst.at[part, mine], recv_sem.at[part]).start()
    for peer in peers:
        pltpu.make_async_remote_copy(
            src_ref=src.at[part, pl.ds(pl.multiple_of(peer * 16, 16), 16)],
            dst_ref=dst.at[part, mine],
            send_sem=send_sem.at[part],
            recv_sem=recv_sem.at[part],
            device_id=(peer, ch),
            device_id_type=MESH,
        ).start()


def arrived(dst, part, recv_sem):
    pltpu.make_async_copy(dst.at[part], dst.at[part], recv_sem.at[part]).wait()


def sent(src, part, send_sem):
    piece = src.at[part, pl.ds(0, 16 * (BLOCKS - 1))]
    pltpu.make_async_copy(piece, piece, send_sem.at[part]).wait()


def lanes_of(block):
    return pl.ds(pl.multiple_of(block * LANES, LANES), LANES)


def short_conv(full, taps, block):
    at = lanes_of(block)
    return (
        taps[0:1, at] * full[8 : 8 + TOK, at]
        + taps[1:2, at] * full[7 : 7 + TOK, at]
        + taps[2:3, at] * full[6 : 6 + TOK, at]
    )


def split_rows(tokens, block, dst):
    first, second = tokens[:LANES].T, tokens[LANES:].T
    for group in range(LANES // C):
        rows = slice(C * group, C * group + C)
        pair = jnp.concatenate([first[rows], second[rows]], axis=0).astype(BF)
        owner = lax.rem(block, 2) * (LANES // C) + group
        dst[block // 2, pl.ds(pl.multiple_of(owner * 16, 16), 16), :] = pair


def make_left(c, slot, taps, left):
    lane = lax.broadcasted_iota(jnp.int32, (8, LANES), 1)
    for u in range(8):
        here = taps[pl.ds((1 + 8 * u) * C + c, 8, stride=C), :]
        before = taps[pl.ds(8 * u * C + c, 8, stride=C), :]
        phases = []
        for r in range(4):
            by = 32 * (3 - r)
            if by:
                phases.append(pltpu.roll(jnp.where(lane >= LANES - by, before, here), by, 1))
            else:
                phases.append(here)
        left[slot, 32 + 32 * u : 64 + 32 * u, :] = jnp.concatenate(phases, axis=0).astype(BF)
        if u % 2:
            yield


def make_right(c, slot, flipped, right):
    lane = lax.broadcasted_iota(jnp.int32, (8, LANES), 1)
    row = lax.broadcasted_iota(jnp.int32, (8, LANES), 0)
    masks = [lane < 31 - 8 * o - row for o in range(4)]
    before = jnp.broadcast_to(flipped[pl.ds(c, 1), :], (8, LANES))
    for m in range(SEGS):
        b, g = m // 8, m % 8
        here = jnp.broadcast_to(flipped[pl.ds((m + 1) * C + c, 1), :], (8, LANES))
        phases = [
            pltpu.roll(
                jnp.where(masks[o], before, here), 97 + 8 * o, 1, stride=1, stride_axis=0
            )
            for o in range(4)
        ]
        half = LANES * (b % 2)
        right[slot, b // 2, 32 * g : 32 * g + 32, half : half + LANES] = jnp.concatenate(
            phases, axis=0
        ).astype(BF)
        before = here
        if m % 16 == 15:
            yield


def multiply(slot, left, right, sums):
    total = None
    for k in range(4):
        n = 256 - 64 * k
        lhs = jnp.concatenate([left[slot, 32 : 32 + n, :], left[slot, 0:n, :]], axis=1)
        part = lax.dot_general(lhs, right[slot, k], NT, preferred_element_type=F32)
        if total is None:
            total = [part[64 * i : 64 * i + 64] for i in range(4)]
        else:
            for i in range(k, 4):
                total[i] = total[i] + part[64 * (i - k) : 64 * (i - k) + 64]
        if k < 3:
            yield
    for u in range(8):
        for r in range(4):
            at = 32 * (u % 2) + 8 * r
            sums[slot, r, 12 + 8 * u : 20 + 8 * u, LANES:] = total[u // 2][at : at + 8, LANES:]
    for u in range(8):
        for r in range(4):
            at = 32 * (u % 2) + 8 * r
            rows = slice(8 + 8 * u, 16 + 8 * u)
            sums[slot, r, rows, 0:LANES] = (
                total[u // 2][at : at + 8, 0:LANES] + sums[slot, r, rows, LANES:]
            )
    yield


def fold(c, slot, skip, sums, plain, result):
    lane = lax.broadcasted_iota(jnp.int32, (8, LANES), 1)
    for u in range(8):
        y = None
        for d in range(4):
            v = None
            for j in range(4):
                r = (j + d) % 4
                w = sums[slot, r, 8 + 8 * u - j : 16 + 8 * u - j, 0:LANES]
                v = w if v is None else jnp.where(lane >= 32 * j, w, v)
            if d:
                v = pltpu.roll(v, 32 * d, 1)
            y = v if y is None else y + v
        at = pl.ds(8 * u * C + c, 8, stride=C)
        result[at, :] = y + skip * plain[at, :]
        if u % 2:
            yield


def kernel(
    gate_hbm, key_hbm, value_hbm, filter_hbm,
    gate_short, key_short, value_short, skip_gain, norm_gain,
    out,
    gate_in, key_in, value_in, filter_in, load_sem,
    gate_full, key_full, value_full,
    edge_out, edge_in, edge_send, edge_recv,
    filter_send, filter_recv, product_send, product_recv, mixed_send, mixed_recv,
    sems,
    gated, taps, plain, flipped, result, left, right, sums,
    square_send, square_recv, square_sems, turned,
    key_tail, value_tail, gate_tail, tail_sem,
):
    me, ch = lax.axis_index("seq"), lax.axis_index("ch")
    tails = [
        pltpu.make_async_copy(src.at[pl.ds(TOK - 16, 16)], dst, tail_sem.at[i])
        for i, (src, dst) in enumerate(
            ((key_hbm, key_tail), (value_hbm, value_tail), (gate_hbm, gate_tail))
        )
    ]
    loads = [
        pltpu.make_async_copy(src, dst, load_sem.at[i])
        for i, (src, dst) in enumerate(
            ((filter_hbm, filter_in), (key_hbm, key_in), (value_hbm, value_in), (gate_hbm, gate_in))
        )
    ]
    for load in tails + loads:
        load.start()

    barrier = pltpu.get_barrier_semaphore()

    peers = others(me)
    for peer in peers:
        pl.semaphore_signal(barrier, inc=1, device_id=(peer, ch), device_id_type=MESH)
    for d in range(1, GROUPS):
        pl.semaphore_signal(
            barrier, inc=1, device_id=(me, lax.rem(ch + d, GROUPS)), device_id_type=MESH
        )

    for load in tails:
        load.wait()
    edge_out[...] = jnp.zeros_like(edge_out)
    for i, tail in enumerate((key_tail, value_tail, gate_tail)):
        edge_out[2 * i : 2 * i + 2, :] = tail[...].astype(F32)[14:16]

    pl.semaphore_wait(barrier, BLOCKS - 1 + GROUPS - 1)
    edge = pltpu.make_async_remote_copy(
        src_ref=edge_out,
        dst_ref=edge_in,
        send_sem=edge_send,
        recv_sem=edge_recv,
        device_id=(lax.rem(me + 1, BLOCKS), ch),
        device_id_type=MESH,
    )
    edge.start()
    loads[0].wait()

    def cut_filter(block, carry):
        split_rows(filter_in[:, lanes_of(block)].astype(F32), block, filter_send)
        return carry

    filter_sems, product_sems, mixed_sems = (
        (sems.at[2 * i], sems.at[2 * i + 1]) for i in range(3)
    )
    lax.fori_loop(0, 2, cut_filter, 0)
    exchange(me, ch, peers, filter_send, filter_recv, 0, *filter_sems)

    for load in loads[1:]:
        load.wait()
    edge.wait()
    for i, full in enumerate((key_full, value_full, gate_full)):
        full[6:8, :] = jnp.where(me == 0, 0.0, edge_in[2 * i : 2 * i + 2, :])

    def cut_product(block, carry):
        at = lanes_of(block)
        key_full[8 : 8 + TOK, at] = key_in[:, at].astype(F32)
        value_full[8 : 8 + TOK, at] = value_in[:, at].astype(F32)
        product = short_conv(key_full, key_short, block) * short_conv(
            value_full, value_short, block
        )
        split_rows(product.astype(BF).astype(F32), block, product_send)
        return carry

    lax.fori_loop(0, 2, cut_product, 0)
    exchange(me, ch, peers, product_send, product_recv, 0, *product_sems)

    def exchange_both(part, carry):
        lax.fori_loop(2 * part, 2 * part + 2, cut_filter, 0)
        exchange(me, ch, peers, filter_send, filter_recv, part, *filter_sems)
        lax.fori_loop(2 * part, 2 * part + 2, cut_product, 0)
        exchange(me, ch, peers, product_send, product_recv, part, *product_sems)
        return carry

    def turn_gate(block, carry):
        at = lanes_of(block)
        gate_full[8 : 8 + TOK, at] = gate_in[:, at].astype(F32)
        gate = short_conv(gate_full, gate_short, block)
        gated[lanes_of(block), 0:LANES] = gate[:LANES].T
        gated[lanes_of(block), LANES : 2 * LANES] = gate[LANES:].T
        return carry

    lax.fori_loop(1, PARTS, exchange_both, 0)

    taps[0:C, :] = jnp.zeros((C, LANES), F32)
    flipped[0:C, :] = jnp.zeros((C, LANES), F32)
    for slot in range(SLOTS):
        left[slot, 0:32, :] = jnp.zeros((32, LANES), BF)
        for r in range(4):
            sums[slot, r, 0:16, :] = jnp.zeros((16, 2 * LANES), F32)
    rows = lax.broadcasted_iota(jnp.int32, (LANES, LANES), 0)
    cols = lax.broadcasted_iota(jnp.int32, (LANES, LANES), 1)
    flip = jnp.where(rows + cols == LANES - 1, 1.0, 0.0).astype(BF)

    def convolve(part, carry):
        arrived(filter_recv, part, filter_sems[1])
        taps[C:, :] = filter_recv[part].astype(F32)
        arrived(product_recv, part, product_sems[1])
        plain[...] = product_recv[part].astype(F32)
        flipped[C:, :] = jnp.dot(product_recv[part], flip, preferred_element_type=F32)

        def channels(i, carry):
            work = []
            for slot in range(SLOTS):
                c = i * SLOTS + slot
                skip = skip_gain[part * (BLOCKS * C) + me * C + c]
                work.append(
                    (
                        (make_left(c, slot, taps, left), make_right(c, slot, flipped, right)),
                        (multiply(slot, left, right, sums),),
                        (fold(c, slot, skip, sums, plain, result),),
                    )
                )
            for beat in range(SLOTS + 2):
                turns = [
                    steps
                    for stage in STAGES
                    if 0 <= beat - stage < SLOTS
                    for steps in work[beat - stage][stage]
                ]
                for _ in range(4):
                    for steps in turns:
                        next(steps, None)
            return carry

        lax.fori_loop(0, C // SLOTS, channels, 0)
        mixed_send[part] = result[...].astype(BF)
        exchange(me, ch, peers, mixed_send, mixed_recv, part, *mixed_sems)
        return carry

    lax.fori_loop(0, PARTS, convolve, 0)
    lax.fori_loop(0, WIDTH // LANES, turn_gate, 0)

    def gate_part(part, squares):
        arrived(mixed_recv, part, mixed_sems[1])

        def gate_owner(owner, squares):
            pair = mixed_recv[part, pl.ds(pl.multiple_of(owner * 16, 16), 16), :].astype(F32)
            at = pl.ds(pl.multiple_of(part * (BLOCKS * C) + owner * C, C), C)
            g = gated[at, :] * jnp.concatenate([pair[:C], pair[C:]], axis=1)
            gated[at, :] = g
            return squares + g * g

        return lax.fori_loop(0, BLOCKS, gate_owner, squares, unroll=4)

    squares = lax.fori_loop(0, PARTS, gate_part, jnp.zeros((C, TOK), F32))
    square_send[...] = squares
    tells = [
        pltpu.make_async_remote_copy(
            src_ref=square_send,
            dst_ref=square_recv.at[d - 1],
            send_sem=square_sems.at[0, d - 1],
            recv_sem=square_sems.at[1, d - 1],
            device_id=(me, lax.rem(ch + d, GROUPS)),
            device_id_type=MESH,
        )
        for d in range(1, GROUPS)
    ]
    for tell in tells:
        tell.start()

    def turn_back(block, carry):
        at = lanes_of(block)
        turned[:, at] = gated[at, :].T * norm_gain[0:1, at]
        return carry

    lax.fori_loop(0, WIDTH // LANES, turn_back, 0)
    for tell in tells:
        tell.wait()
    for d in range(GROUPS - 1):
        squares = squares + square_recv[d]
    meansq = jnp.sum(squares, axis=0, keepdims=True) / (WIDTH * GROUPS)
    inverse = lax.rsqrt(meansq + 1e-06)
    scale = jnp.broadcast_to(inverse, (LANES, TOK)).T

    for block in range(WIDTH // LANES):
        at = slice(LANES * block, LANES * block + LANES)
        out[:, at] = (turned[:, at] * scale).astype(BF)

    edge_free = [(filter_send, filter_sems), (product_send, product_sems), (mixed_send, mixed_sems)]
    for src, pair in edge_free:
        for part in range(PARTS):
            sent(src, part, pair[0])


def local(
    gate_in, key_in, value_in, long_filter, gate_short, key_short, value_short, skip_gain, norm_gain
):
    vmem = pl.BlockSpec(memory_space=pltpu.VMEM)
    smem = pl.BlockSpec(memory_space=pltpu.SMEM)
    hbm = pl.BlockSpec(memory_space=pl.ANY)
    parts = (PARTS, ROWS, LANES)
    return pl.pallas_call(
        kernel,
        out_shape=jax.ShapeDtypeStruct((TOK, WIDTH), BF),
        in_specs=[hbm] * 4 + [vmem] * 3 + [smem, vmem],
        out_specs=vmem,
        scratch_shapes=[
            *[pltpu.VMEM((TOK, WIDTH), BF)] * 4,
            pltpu.SemaphoreType.DMA((4,)),
            *[pltpu.VMEM((8 + TOK, WIDTH), F32)] * 3,
            *[pltpu.VMEM((8, WIDTH), F32)] * 2,
            pltpu.SemaphoreType.DMA,
            pltpu.SemaphoreType.DMA,
            *[pltpu.VMEM(parts, BF)] * 6,
            pltpu.SemaphoreType.DMA((6, PARTS)),
            pltpu.VMEM((WIDTH, TOK), F32),
            pltpu.VMEM((ROWS + C, LANES), F32),
            pltpu.VMEM((ROWS, LANES), F32),
            pltpu.VMEM((ROWS + C, LANES), F32),
            pltpu.VMEM((ROWS, LANES), F32),
            pltpu.VMEM((SLOTS, 288, LANES), BF),
            pltpu.VMEM((SLOTS, 4, 256, 256), BF),
            pltpu.VMEM((SLOTS, 4, 80, 256), F32),
            pltpu.VMEM((C, TOK), F32),
            pltpu.VMEM((GROUPS - 1, C, TOK), F32),
            pltpu.SemaphoreType.DMA((2, GROUPS - 1)),
            pltpu.VMEM((TOK, WIDTH), F32),
            *[pltpu.VMEM((16, WIDTH), BF)] * 3,
            pltpu.SemaphoreType.DMA((3,)),
        ],
        compiler_params=pltpu.CompilerParams(
            collective_id=0, has_side_effects=True, vmem_limit_bytes=60 << 20
        ),
        name="hyena",
    )(
        gate_in, key_in, value_in, long_filter,
        gate_short, key_short, value_short, skip_gain, norm_gain.reshape(1, WIDTH),
    )


def solution(mesh):
    return jax.shard_map(
        local,
        mesh=mesh,
        in_specs=(
            P("seq", "ch"),
            P("seq", "ch"),
            P("seq", "ch"),
            P("seq", "ch"),
            P(None, "ch"),
            P(None, "ch"),
            P(None, "ch"),
            P("ch"),
            P("ch"),
        ),
        out_specs=P("seq", "ch"),
        check_vma=False,
    )
```
